256 devices in a mesh: seq: 128 (over x, y, z), head: 2 (over core).
Axes of the slice: x: 4, y: 4, z: 8, core: 2. Of those that a mesh axis runs over, the one named last changes fastest.
Arguments:
- query_rows: bfloat16 [131072, 16, 128], P('seq', 'head'), may hold values from -1.796875 to 1.796875
- key_rows: bfloat16 [131072, 16, 128], P('seq', 'head'), may hold values from -1.796875 to 1.796875
- value_rows: bfloat16 [131072, 16, 128], P('seq', 'head'), may hold values from -6 to 6
- level_codes: int32 [16, 18, 131072], P('head', None, 'seq'), may hold values from 0 to 63
- norm_gain: float32 [16, 128], P('head'), may hold values from 0.1 to 1.9
Outputs:
- normed: bfloat16 [131072, 16, 128], P('seq', 'head')
The draws below stay inside these ranges and needn't reach their ends.
All inputs are finite; a program needn't handle non-finite values.
Results may differ from the reference program's by a relative error of at most 0.0022.
Values sent between devices are 32-bit elements; how exact they have to be, the bound alone decides.
No kernel may reach another device: no remote copies, remote signals or barrier semaphores. Data moves between devices by JAX's collectives and lax.ppermute only.
A program may use at most 128 MiB of HBM per device.

```python
import jax
import jax.numpy as jnp
import numpy as np
from jax import lax

HEADS = 16
HEAD_DIM = 128
SEQ_DEV = 1024
LENGTH = 131072
LOCAL_BITS = 10
SEQ_BITS = 7
LEVELS = 18
N_SEQ = 128


def set_ends(values, stream_key, smallest, top_value):
    spot = [jax.random.randint(jax.random.fold_in(stream_key, axis), (), 0, length) for axis, length in enumerate(values.shape)]
    main_axis = values.shape.index(max(values.shape))
    neighbour = spot[:main_axis] + [(spot[main_axis] + 1) % values.shape[main_axis]] + spot[main_axis + 1:]
    return values.at[tuple(spot)].set(smallest).at[tuple(neighbour)].set(top_value)


def block_scale(rng, extent, split, low, largest):
    gain = 1.0
    for axis_at, blocks in split:
        heights = jax.random.uniform(jax.random.fold_in(jax.random.fold_in(rng, 6), axis_at), (blocks,), jnp.float32, low / len(split), largest / len(split))
        gain = gain * jnp.repeat(jnp.exp(heights), extent[axis_at] // blocks).reshape((-1,) + (1,) * (len(extent) - 1 - axis_at))
    return gain


def scatter_about(rng, extent, width, most, pieces=(), kind=jnp.bfloat16):
    values = width * jax.random.normal(rng, extent, jnp.float32)
    if pieces:
        values = values * block_scale(rng, extent, pieces, -0.22, 0.18)
    return jnp.clip(values, -most, most).astype(kind)


def setup_inputs(seed: int = 0) -> dict:
    arg_keys = jax.random.split(jax.random.key(seed), 6)
    query_rows = scatter_about(arg_keys[0], (LENGTH, HEADS, HEAD_DIM), 0.3, 1.796875, ((0, 128), (1, 2)))
    key_rows = scatter_about(arg_keys[1], (LENGTH, HEADS, HEAD_DIM), 0.3, 1.796875, ((0, 128), (1, 2)))
    value_rows = scatter_about(arg_keys[2], (LENGTH, HEADS, HEAD_DIM), 1.0, 6.0, ((0, 128), (1, 2)))
    level_codes = set_ends(jax.random.randint(arg_keys[3], (HEADS, LEVELS, LENGTH), 0, 64), jax.random.fold_in(arg_keys[3], 1), 0, 63).astype(jnp.int32)
    norm_gain = jnp.clip(1.0 + 0.18 * jax.random.normal(arg_keys[4], (HEADS, HEAD_DIM), jnp.float32), 0.1, 1.9)
    return {"query_rows": query_rows, "key_rows": key_rows, "value_rows": value_rows, "level_codes": level_codes, "norm_gain": norm_gain}


def level_table(length_dev):
    target = np.arange(length_dev)[:, None]
    source = np.arange(length_dev)[None, :]
    levels = np.zeros((length_dev, length_dev), np.int32)
    for shift_count in range(24):
        levels = levels + (target >> shift_count != source >> shift_count).astype(np.int32)
    return levels

def reference(query_rows, key_rows, value_rows, level_codes, norm_gain):
    level_map = jnp.asarray(level_table(SEQ_DEV))
    level_index = jnp.broadcast_to(level_map[None], (HEADS, SEQ_DEV, SEQ_DEV))
    causal = jnp.asarray(np.tril(np.ones((SEQ_DEV, SEQ_DEV), np.int32)) > 0)
    weights = level_codes.astype(jnp.float32) / 64.0
    query_blocks = query_rows.reshape(N_SEQ, SEQ_DEV, HEADS, HEAD_DIM)
    key_blocks = key_rows.reshape(N_SEQ, SEQ_DEV, HEADS, HEAD_DIM)
    value_blocks = value_rows.reshape(N_SEQ, SEQ_DEV, HEADS, HEAD_DIM)
    weight_blocks = jnp.moveaxis(weights.reshape(HEADS, LEVELS, N_SEQ, SEQ_DEV), 2, 0)

    def block_state(pair):
        return jnp.einsum('shd,she->hde', pair[0].astype(jnp.float32), pair[1].astype(jnp.float32))
    states = lax.map(block_state, (key_blocks, value_blocks))

    def one_block(inputs):
        block_index, queries, block_keys, block_values, block_weights = inputs
        scores = jnp.einsum('thd,shd->hts', queries.astype(jnp.float32), block_keys.astype(jnp.float32))
        picked = jnp.take_along_axis(jnp.swapaxes(block_weights, 1, 2), level_index, axis=2)
        weighted = jnp.where(causal[None], picked * scores, 0.0).astype(jnp.bfloat16)
        local_part = jnp.einsum('hts,she->the', weighted.astype(jnp.float32), block_values.astype(jnp.float32))
        cross_part = jnp.zeros((SEQ_DEV, HEADS, HEAD_DIM), jnp.float32)
        for level_bit in range(SEQ_BITS):
            width_blocks = 2 ** level_bit
            start = (block_index // (2 * width_blocks) * (2 * width_blocks)).astype(jnp.int32)
            bucket = lax.optimization_barrier(jnp.sum(lax.dynamic_slice_in_dim(states, start, width_blocks, 0), axis=0))
            product = jnp.einsum('thd,hde->the', queries.astype(jnp.float32), bucket, precision=lax.Precision.HIGHEST)
            bit_flag = (block_index // width_blocks % 2).astype(jnp.float32)
            level_scale = block_weights[:, LOCAL_BITS + 1 + level_bit, :].T
            cross_part = cross_part + (bit_flag * level_scale)[:, :, None] * product
        result = local_part + cross_part
        mean_square = lax.optimization_barrier(jnp.mean(result * result, axis=-1, keepdims=True))
        return (result * lax.rsqrt(mean_square + 1e-06) * norm_gain[None]).astype(jnp.bfloat16)
    block_ids = jnp.arange(N_SEQ, dtype=jnp.int32)
    normed = lax.map(one_block, (block_ids, query_blocks, key_blocks, value_blocks, weight_blocks))
    return normed.reshape(LENGTH, HEADS, HEAD_DIM)
```

```python
import functools

import jax
import jax.numpy as jnp
import numpy as np
from jax import lax
from jax.experimental import pallas as pl
from jax.experimental.pallas import tpu as pltpu
from jax.sharding import PartitionSpec as P

VMEM_LIMIT = 40 * 1024 * 1024
NT = (((1,), (1,)), ((), ()))


def params():
    return pltpu.CompilerParams(vmem_limit_bytes=VMEM_LIMIT)


def cost(flops, nbytes):
    return pl.CostEstimate(flops=flops, bytes_accessed=nbytes, transcendentals=0)


def level_map(size):
    source = np.arange(size)[:, None]
    target = np.arange(size)[None, :]
    levels = np.zeros((size, size), np.int32)
    for shift in range(24):
        levels += (target >> shift != source >> shift).astype(np.int32)
    return np.where(source <= target, levels, -1).astype(np.int32)


def states_kernel(heads, rows, k_ref, v_ref, key_out, value_out, state_out, k_wide, v_wide):
    k_wide[...] = k_ref[...].astype(jnp.float32)
    v_wide[...] = v_ref[...].astype(jnp.float32)

    @pl.when(pl.program_id(0) == 0)
    def _():
        state_out[...] = jnp.zeros_like(state_out)

    for h in range(heads):
        key = k_wide[pl.ds(h, rows, stride=heads), :].astype(jnp.bfloat16)
        value = v_wide[pl.ds(h, rows, stride=heads), :].T.astype(jnp.bfloat16)
        key_out[h] = key
        value_out[h] = value
        state_out[h] += jnp.dot(value, key, preferred_element_type=jnp.float32)


def make_states(key_rows, value_rows, rows=256):
    length, heads, dim = key_rows.shape
    flat = pl.BlockSpec((rows * heads, dim), lambda i: (i, 0))
    return pl.pallas_call(
        functools.partial(states_kernel, heads, rows),
        grid=(length // rows,),
        in_specs=[flat, flat],
        out_specs=[
            pl.BlockSpec((heads, rows, dim), lambda i: (0, i, 0)),
            pl.BlockSpec((heads, dim, rows), lambda i: (0, 0, i)),
            pl.BlockSpec((heads, dim, dim), lambda i: (0, 0, 0)),
        ],
        out_shape=[
            jax.ShapeDtypeStruct((heads, length, dim), jnp.bfloat16),
            jax.ShapeDtypeStruct((heads, dim, length), jnp.bfloat16),
            jax.ShapeDtypeStruct((heads, dim, dim), jnp.float32),
        ],
        scratch_shapes=[pltpu.VMEM((rows * heads, dim), jnp.float32)] * 2,
        compiler_params=params(),
        cost_estimate=cost(2 * heads * length * dim * dim, 8 * length * heads * dim),
        name="states",
    )(key_rows.reshape(length * heads, dim), value_rows.reshape(length * heads, dim))


def split_kernel(heads, rows, q_ref, q_out, q_wide):
    q_wide[...] = q_ref[...].astype(jnp.float32)
    for h in range(heads):
        q_out[h] = q_wide[pl.ds(h, rows, stride=heads), :].astype(jnp.bfloat16)


def split_heads(query_rows, rows=256):
    length, heads, dim = query_rows.shape
    return pl.pallas_call(
        functools.partial(split_kernel, heads, rows),
        grid=(length // rows,),
        in_specs=[pl.BlockSpec((rows * heads, dim), lambda i: (i, 0))],
        out_specs=pl.BlockSpec((heads, rows, dim), lambda i: (0, i, 0)),
        out_shape=jax.ShapeDtypeStruct((heads, length, dim), jnp.bfloat16),
        scratch_shapes=[pltpu.VMEM((rows * heads, dim), jnp.float32)],
        compiler_params=params(),
        cost_estimate=cost(0, 4 * length * heads * dim),
        name="split_heads",
    )(query_rows.reshape(length * heads, dim))


def local_kernel(length, tile, small, q_ref, k_ref, v_ref, codes_ref, map_ref, out_ref):
    weights = codes_ref[0].astype(jnp.float32) * (1.0 / 64.0)
    low_levels = small.bit_length()
    levels = map_ref[...]
    masks = [levels == level for level in range(low_levels)]
    for t in range(length // tile):
        columns = slice(t * tile, (t + 1) * tile)
        count = (t + 1) * tile
        scores = lax.dot_general(
            k_ref[0, :count, :], q_ref[0, columns, :], NT, preferred_element_type=jnp.float32
        )
        pieces = []
        for s in range(t):
            level = (t ^ s).bit_length() + tile.bit_length() - 1
            piece = scores[s * tile:(s + 1) * tile] * weights[level:level + 1, columns]
            pieces.append(piece.astype(jnp.bfloat16))
        for i in range(tile // small):
            row = []
            for j in range(tile // small):
                first = t * tile + j * small
                lanes = slice(first, first + small)
                part = scores[t * tile + i * small:t * tile + (i + 1) * small, j * small:(j + 1) * small]
                if j < i:
                    row.append(jnp.zeros((small, small), jnp.bfloat16))
                    continue
                if j > i:
                    level = (i ^ j).bit_length() + small.bit_length() - 1
                    picked = weights[level:level + 1, lanes]
                else:
                    picked = jnp.zeros((small, small), jnp.float32)
                    for level in range(low_levels):
                        picked = jnp.where(masks[level], weights[level:level + 1, lanes], picked)
                row.append((part * picked).astype(jnp.bfloat16))
            pieces.append(jnp.concatenate(row, axis=1))
        weighted = jnp.concatenate(pieces, axis=0) if len(pieces) > 1 else pieces[0]
        out_ref[0, :, columns] = jnp.dot(
            v_ref[0, :, :count], weighted, preferred_element_type=jnp.float32
        )


def local_part(query, key, value, codes, tile=256, small=128):
    heads, length, dim = query.shape
    levels = codes.shape[1]
    return pl.pallas_call(
        functools.partial(local_kernel, length, tile, small),
        grid=(heads,),
        in_specs=[
            pl.BlockSpec((1, length, dim), lambda h: (h, 0, 0)),
            pl.BlockSpec((1, length, dim), lambda h: (h, 0, 0)),
            pl.BlockSpec((1, dim, length), lambda h: (h, 0, 0)),
            pl.BlockSpec((1, levels, length), lambda h: (h, 0, 0)),
            pl.BlockSpec((small, small), lambda h: (0, 0)),
        ],
        out_specs=pl.BlockSpec((1, dim, length), lambda h: (h, 0, 0)),
        out_shape=jax.ShapeDtypeStruct((heads, dim, length), jnp.float32),
        compiler_params=params(),
        cost_estimate=cost(16 * heads * length * length * dim, 16 * length * heads * dim),
        name="local_part",
    )(query, key, value, codes, jnp.asarray(level_map(small)))


def bucket_product(bucket, query):
    high = bucket.astype(jnp.bfloat16)
    low = (bucket - high.astype(jnp.float32)).astype(jnp.bfloat16)
    both = lax.dot_general(
        jnp.concatenate([high, low], axis=0), query, NT, preferred_element_type=jnp.float32
    )
    dim = bucket.shape[0]
    return both[:dim] + both[dim:]


def cross_kernel(bits, first, total_ref, q_ref, codes_ref, flag_ref, *refs):
    out_ref = refs[-1]
    total = total_ref[0]
    for bit, bucket_ref in zip(bits, refs[:-1]):
        scale = codes_ref[0, first + bit:first + bit + 1, :].astype(jnp.float32) * flag_ref[bit]
        total = total + scale * bucket_product(bucket_ref[0], q_ref[0])
    out_ref[0] = total


def add_cross(total, query, codes, flags, buckets, bits, first):
    heads, length, dim = query.shape
    levels = codes.shape[1]
    return pl.pallas_call(
        functools.partial(cross_kernel, bits, first),
        grid=(heads,),
        in_specs=[
            pl.BlockSpec((1, dim, length), lambda h: (h, 0, 0)),
            pl.BlockSpec((1, length, dim), lambda h: (h, 0, 0)),
            pl.BlockSpec((1, levels, length), lambda h: (h, 0, 0)),
            pl.BlockSpec(memory_space=pltpu.SMEM),
        ] + [pl.BlockSpec((1, dim, dim), lambda h: (h, 0, 0))] * len(bits),
        out_specs=pl.BlockSpec((1, dim, length), lambda h: (h, 0, 0)),
        out_shape=jax.ShapeDtypeStruct((heads, dim, length), jnp.float32),
        input_output_aliases={0: 0},
        compiler_params=params(),
        cost_estimate=cost(8 * len(bits) * heads * length * dim * dim, 12 * length * heads * dim),
        name="add_cross",
    )(total, query, codes, flags, *buckets)


def finish_kernel(bits, first, total_ref, q_ref, codes_ref, flag_ref, gain_ref, *refs):
    out_ref, wide = refs[-2:]
    heads, dim, rows = total_ref.shape
    for h in range(heads):
        total = total_ref[h]
        for bit, bucket_ref in zip(bits, refs[:-2]):
            scale = codes_ref[h, first + bit:first + bit + 1, :].astype(jnp.float32) * flag_ref[bit]
            total = total + scale * bucket_product(bucket_ref[h], q_ref[h])
        mean_square = jnp.sum(total * total, axis=0, keepdims=True) * (1.0 / dim)
        normed = total * lax.rsqrt(mean_square + 1e-06)
        wide[pl.ds(h, rows, stride=heads), :] = normed.T * gain_ref[h:h + 1, :]
    out_ref[...] = wide[...].astype(jnp.bfloat16)


def finish(total, query, codes, flags, gain, buckets, bits, first, rows=256):
    heads, length, dim = query.shape
    levels = codes.shape[1]
    out = pl.pallas_call(
        functools.partial(finish_kernel, bits, first),
        grid=(length // rows,),
        in_specs=[
            pl.BlockSpec((heads, dim, rows), lambda i: (0, 0, i)),
            pl.BlockSpec((heads, rows, dim), lambda i: (0, i, 0)),
            pl.BlockSpec((heads, levels, rows), lambda i: (0, 0, i)),
            pl.BlockSpec(memory_space=pltpu.SMEM),
            pl.BlockSpec((heads, dim), lambda i: (0, 0)),
        ] + [pl.BlockSpec((heads, dim, dim), lambda i: (0, 0, 0))] * len(bits),
        out_specs=pl.BlockSpec((rows * heads, dim), lambda i: (i, 0)),
        out_shape=jax.ShapeDtypeStruct((length * heads, dim), jnp.bfloat16),
        scratch_shapes=[pltpu.VMEM((rows * heads, dim), jnp.float32)],
        compiler_params=params(),
        cost_estimate=cost(8 * heads * length * dim * dim, 10 * length * heads * dim),
        name="finish",
    )(total, query, codes, flags, gain, *buckets)
    return out.reshape(length, heads, dim)


def swapped(block, mask):
    count = lax.axis_size("seq")
    return lax.ppermute(block, "seq", [(i, i ^ mask) for i in range(count)])


MASKS = (1, 3, 7, 8, 24, 32, 96)


def shards(query_rows, key_rows, value_rows, level_codes, norm_gain):
    first = level_codes.shape[1] - len(MASKS)
    position = lax.axis_index("seq")
    bits = jnp.arange(len(MASKS), dtype=jnp.int32)
    flags = (position >> bits & 1).astype(jnp.float32) * (1.0 / 64.0)
    key, value, states = make_states(key_rows, value_rows)
    buckets = []
    block_sum = states
    for mask in MASKS:
        partner = swapped(block_sum, mask)
        buckets.append(partner)
        block_sum = block_sum + partner
    query = split_heads(query_rows)
    total = local_part(query, key, value, level_codes)
    total = add_cross(total, query, level_codes, flags, buckets[:3], (0, 1, 2), first)
    total = add_cross(total, query, level_codes, flags, buckets[3:6], (3, 4, 5), first)
    return finish(total, query, level_codes, flags, norm_gain, buckets[6:], (6,), first)


def solution(mesh):
    return jax.shard_map(
        shards,
        mesh=mesh,
        in_specs=(
            P("seq", "head", None),
            P("seq", "head", None),
            P("seq", "head", None),
            P("head", None, "seq"),
            P("head", None),
        ),
        out_specs=P("seq", "head", None),
        check_vma=False,
    )
```

```python
import functools

import jax
import jax.numpy as jnp
import numpy as np
from jax import lax
from jax.experimental import pallas as pl
from jax.experimental.pallas import tpu as pltpu
from jax.sharding import PartitionSpec as P

STATES_MIB = 58
NT = (((1,), (1,)), ((), ()))
VMEM = pl.BlockSpec(memory_space=pltpu.VMEM)
SMEM = pl.BlockSpec(memory_space=pltpu.SMEM)
ANY = pl.BlockSpec(memory_space=pl.ANY)


def params(mib):
    return pltpu.CompilerParams(vmem_limit_bytes=mib * 1024 * 1024)


def cost(flops, nbytes):
    return pl.CostEstimate(flops=flops, bytes_accessed=nbytes, transcendentals=0)


def level_map(size):
    source = np.arange(size)[:, None]
    target = np.arange(size)[None, :]
    levels = np.zeros((size, size), np.int32)
    for shift in range(24):
        levels += (target >> shift != source >> shift).astype(np.int32)
    return np.where(source <= target, levels, -1).astype(np.int32)


def first_head(owner_ref, own_heads, half):
    return (owner_ref[0] if own_heads else 1 - owner_ref[0]) * half


def states_kernel(heads, rows, owner_ref, k_hbm, v_hbm, own_out, other_out, k_in, v_in, k_wide, v_wide, state, sems):
    chunks = k_in.shape[0]
    half = heads // 2

    def load(hbm, buffer, which, i):
        part = pl.ds(i * rows * heads, rows * heads)
        return pltpu.make_async_copy(hbm.at[part], buffer.at[i], sems.at[which, i])

    for i in range(chunks):
        load(k_hbm, k_in, 0, i).start()
        load(v_hbm, v_in, 1, i).start()
    for i in range(chunks):
        load(k_hbm, k_in, 0, i).wait()
        load(v_hbm, v_in, 1, i).wait()
        k_wide[...] = k_in[i].astype(jnp.float32)
        v_wide[...] = v_in[i].astype(jnp.float32)
        for h in range(heads):
            key = k_wide[pl.ds(h, rows, stride=heads), :].astype(jnp.bfloat16)
            value = v_wide[pl.ds(h, rows, stride=heads), :].T.astype(jnp.bfloat16)
            product = jnp.dot(value, key, preferred_element_type=jnp.float32)
            if i:
                product = state[h] + product
            state[h] = product
    owner = owner_ref[0]
    own_out[...] = state[pl.ds(owner * half, half)]
    other_out[...] = state[pl.ds((1 - owner) * half, half)]


def make_states(key_rows, value_rows, owner, rows=128):
    length, heads, dim = key_rows.shape
    chunks = length // rows
    part = jax.ShapeDtypeStruct((heads // 2, dim, dim), jnp.float32)
    return pl.pallas_call(
        functools.partial(states_kernel, heads, rows),
        in_specs=[SMEM, ANY, ANY],
        out_specs=[VMEM, VMEM],
        out_shape=[part, part],
        scratch_shapes=[pltpu.VMEM((chunks, rows * heads, dim), jnp.bfloat16)] * 2
        + [pltpu.VMEM((rows * heads, dim), jnp.float32)] * 2
        + [pltpu.VMEM((heads, dim, dim), jnp.float32)]
        + [pltpu.SemaphoreType.DMA((2, chunks))],
        compiler_params=params(STATES_MIB),
        cost_estimate=cost(2 * heads * length * dim * dim, 4 * length * heads * dim),
        name="states",
    )(owner, key_rows.reshape(length * heads, dim), value_rows.reshape(length * heads, dim))


def split_kernel(heads, rows, _, q_ref, k_ref, v_ref, q_out, k_out, v_out, q_wide, k_wide, v_wide):
    for i in range(q_out.shape[1] // rows):
        span = slice(i * rows, (i + 1) * rows)
        flat = slice(i * rows * heads, (i + 1) * rows * heads)
        q_wide[...] = q_ref[flat, :].astype(jnp.float32)
        k_wide[...] = k_ref[flat, :].astype(jnp.float32)
        v_wide[...] = v_ref[flat, :].astype(jnp.float32)
        for h in range(heads):
            q_out[h, span, :] = q_wide[pl.ds(h, rows, stride=heads), :].astype(jnp.bfloat16)
            k_out[h, span, :] = k_wide[pl.ds(h, rows, stride=heads), :].astype(jnp.bfloat16)
            v_out[h, :, span] = v_wide[pl.ds(h, rows, stride=heads), :].T.astype(jnp.bfloat16)


def split_heads(earlier, query_rows, key_rows, value_rows, rows=256):
    length, heads, dim = query_rows.shape
    straight = jax.ShapeDtypeStruct((heads, length, dim), jnp.bfloat16)
    turned = jax.ShapeDtypeStruct((heads, dim, length), jnp.bfloat16)
    return pl.pallas_call(
        functools.partial(split_kernel, heads, rows),
        in_specs=[ANY] + [VMEM] * 3,
        out_specs=[VMEM] * 3,
        out_shape=[straight, straight, turned],
        scratch_shapes=[pltpu.VMEM((rows * heads, dim), jnp.float32)] * 3,
        compiler_params=params(12),
        cost_estimate=cost(0, 12 * length * heads * dim),
        name="split_heads",
    )(earlier, *[each.reshape(length * heads, dim) for each in (query_rows, key_rows, value_rows)])


def local_kernel(length, tile, small, own_heads, owner_ref, q_ref, k_ref, v_ref, codes_ref, map_ref, *refs):
    out_ref = refs[-1]
    low_levels = small.bit_length()

    half = q_ref.shape[0] // 2
    begin = first_head(owner_ref, own_heads, half)

    @pl.loop(0, half)
    def _(i):
        h = begin + i
        weights = [codes_ref[level, pl.ds(h, 1), :].astype(jnp.float32) * (1.0 / 64.0) for level in range(length.bit_length())]
        levels = map_ref[...]
        masks = [levels == level for level in range(low_levels)]
        for t in range(length // tile):
            columns = slice(t * tile, (t + 1) * tile)
            count = (t + 1) * tile
            scores = lax.dot_general(
                k_ref[h, :count, :], q_ref[h, columns, :], NT, preferred_element_type=jnp.float32
            )
            pieces = []
            for s in range(t):
                level = (t ^ s).bit_length() + tile.bit_length() - 1
                piece = scores[s * tile:(s + 1) * tile] * weights[level][:, columns]
                pieces.append(piece.astype(jnp.bfloat16))
            for i in range(tile // small):
                row = []
                for j in range(tile // small):
                    first = t * tile + j * small
                    lanes = slice(first, first + small)
                    part = scores[t * tile + i * small:t * tile + (i + 1) * small, j * small:(j + 1) * small]
                    if j < i:
                        row.append(jnp.zeros((small, small), jnp.bfloat16))
                        continue
                    if j > i:
                        level = (i ^ j).bit_length() + small.bit_length() - 1
                        picked = weights[level][:, lanes]
                    else:
                        picked = jnp.zeros((small, small), jnp.float32)
                        for level in range(low_levels):
                            picked = jnp.where(masks[level], weights[level][:, lanes], picked)
                    row.append((part * picked).astype(jnp.bfloat16))
                pieces.append(jnp.concatenate(row, axis=1))
            weighted = jnp.concatenate(pieces, axis=0) if len(pieces) > 1 else pieces[0]
            out_ref[h, :, columns] = jnp.dot(
                v_ref[h, :, :count], weighted, preferred_element_type=jnp.float32
            )


def local_part(total, query, key, value, codes, owner, own_heads, tile=256, small=128):
    every, length, dim = query.shape
    operands = [owner, query, key, value, codes, jnp.asarray(level_map(small))]
    specs = [SMEM] + [VMEM] * (len(operands) - 1)
    aliases = {}
    if total is not None:
        aliases = {len(operands): 0}
        operands.append(total)
        specs.append(VMEM)
    return pl.pallas_call(
        functools.partial(local_kernel, length, tile, small, own_heads),
        in_specs=specs,
        out_specs=VMEM,
        out_shape=jax.ShapeDtypeStruct((every, dim, length), jnp.float32),
        input_output_aliases=aliases,
        compiler_params=params(12),
        cost_estimate=cost(5 * every * length * length * dim, 8 * length * every * dim),
        name="local_part",
    )(*operands)


def bucket_products(buckets, query):
    stacked = jnp.concatenate(buckets, axis=0) if len(buckets) > 1 else buckets[0]
    high = stacked.astype(jnp.bfloat16)
    low = (stacked - high.astype(jnp.float32)).astype(jnp.bfloat16)
    products = lax.dot_general(
        jnp.concatenate([high, low], axis=1),
        jnp.concatenate([query, query], axis=1),
        NT,
        preferred_element_type=jnp.float32,
    )
    dim = query.shape[1]
    return [products[i * dim:(i + 1) * dim] for i in range(len(buckets))]


def cross_kernel(bits, first, own_heads, owner_ref, flag_ref, total_ref, q_ref, codes_ref, *refs):
    out_ref = refs[-1]
    half = q_ref.shape[0] // 2
    begin = first_head(owner_ref, own_heads, half)

    @pl.loop(0, half)
    def _(i):
        h = begin + i
        total = total_ref[h]
        products = bucket_products([ref[i] for ref in refs[:-1]], q_ref[h])
        for product, bit in zip(products, bits):
            scale = codes_ref[first + bit, pl.ds(h, 1), :].astype(jnp.float32) * flag_ref[bit]
            total = total + scale * product
        out_ref[h] = total


def add_cross(total, query, codes, flags, owner, own_heads, buckets, bits, first):
    heads, length, dim = query.shape
    return pl.pallas_call(
        functools.partial(cross_kernel, bits, first, own_heads),
        in_specs=[SMEM, SMEM] + [VMEM] * (3 + len(bits)),
        out_specs=VMEM,
        out_shape=jax.ShapeDtypeStruct((heads, dim, length), jnp.float32),
        input_output_aliases={2: 0},
        compiler_params=params(12),
        cost_estimate=cost(3 * len(bits) * heads * length * dim * dim, 3 * length * heads * dim),
        name="add_cross",
    )(owner, flags, total, query, codes, *buckets)


def finish_kernel(bits, first, rows, own_heads, owner_ref, flag_ref, total_ref, q_ref, codes_ref, gain_ref, *refs):
    buckets = refs[:len(bits)]
    if own_heads:
        wide = refs[-1]
    else:
        wide, out_hbm, narrow, sems = refs[-4:]
    heads, dim, length = total_ref.shape
    half = heads // 2
    chunks = length // rows
    begin = first_head(owner_ref, own_heads, half)

    def store(i):
        part = pl.ds(i * rows * heads, rows * heads)
        return pltpu.make_async_copy(narrow.at[i], out_hbm.at[part], sems.at[i])

    for c in range(chunks):
        columns = slice(c * rows, (c + 1) * rows)
        for i in range(half):
            h = begin + i
            total = total_ref[h, :, columns]
            products = bucket_products([ref[i] for ref in buckets], q_ref[h, columns, :])
            for product, bit in zip(products, bits):
                scale = codes_ref[first + bit, pl.ds(h, 1), columns].astype(jnp.float32) * flag_ref[bit]
                total = total + scale * product
            mean_square = jnp.sum(total * total, axis=0, keepdims=True) * (1.0 / dim)
            normed = total * lax.rsqrt(mean_square + 1e-06)
            wide[pl.ds(c * rows * heads + h, rows, stride=heads), :] = normed.T * gain_ref[pl.ds(h, 1), :]
        if not own_heads:
            narrow[c] = wide[c * rows * heads:(c + 1) * rows * heads, :].astype(jnp.bfloat16)
            store(c).start()
    if not own_heads:
        for c in range(chunks):
            store(c).wait()


def finish_own(total, query, codes, flags, owner, gain, buckets, bits, first, rows=256):
    heads, length, dim = query.shape
    return pl.pallas_call(
        functools.partial(finish_kernel, bits, first, rows, True),
        in_specs=[SMEM, SMEM] + [VMEM] * (4 + len(bits)),
        out_specs=VMEM,
        out_shape=jax.ShapeDtypeStruct((length * heads, dim), jnp.float32),
        compiler_params=params(12),
        cost_estimate=cost(4 * heads * length * dim * dim, 4 * length * heads * dim),
        name="finish_own",
    )(owner, flags, total, query, codes, gain, *buckets)


def finish_other(wide, total, query, codes, flags, owner, gain, buckets, bits, first, rows=256):
    heads, length, dim = query.shape
    _, out = pl.pallas_call(
        functools.partial(finish_kernel, bits, first, rows, False),
        in_specs=[SMEM, SMEM] + [VMEM] * (5 + len(bits)),
        out_specs=[VMEM, ANY],
        out_shape=[
            jax.ShapeDtypeStruct((length * heads, dim), jnp.float32),
            jax.ShapeDtypeStruct((length * heads, dim), jnp.bfloat16),
        ],
        scratch_shapes=[
            pltpu.VMEM((length // rows, rows * heads, dim), jnp.bfloat16),
            pltpu.SemaphoreType.DMA((length // rows,)),
        ],
        input_output_aliases={6 + len(bits): 0},
        compiler_params=params(12),
        cost_estimate=cost(4 * heads * length * dim * dim, 10 * length * heads * dim),
        name="finish_other",
    )(owner, flags, total, query, codes, gain, *buckets, wide)
    return out.reshape(length, heads, dim)


def swapped(block, mask):
    count = lax.axis_size("seq")
    return lax.ppermute(block, "seq", [(i, i ^ mask) for i in range(count)])


def next_along_z(block):
    count = lax.axis_size("seq")
    route = []
    for i in range(count):
        ring = i & ~7
        step = 1 if i & 1 else -1
        route.append((i, ring | (i + step) & 7))
    return lax.ppermute(block, "seq", route)


def shards(query_rows, key_rows, value_rows, level_codes, norm_gain):
    bit_count = lax.axis_size("seq").bit_length() - 1
    first = level_codes.shape[1] - bit_count
    position = lax.axis_index("seq")
    bits = jnp.arange(bit_count, dtype=jnp.int32)
    flags = (position >> bits & 1).astype(jnp.float32) * (1.0 / 64.0)
    owner = position & 1
    half_id = owner.reshape(1).astype(jnp.int32)

    codes = jnp.transpose(level_codes, (1, 0, 2))
    own_state, other_state = make_states(key_rows, value_rows, half_id)
    half = own_state.shape[0]

    own0 = swapped(other_state, 1)
    query, key, value = split_heads(own_state, query_rows, key_rows, value_rows)
    own0, own_state, query = lax.optimization_barrier((own0, own_state, query))
    block_sum = own_state + own0

    def local(total, own_heads):
        return local_part(total, query, key, value, codes, half_id, own_heads)

    def cross(total, own_heads, buckets, bits):
        return add_cross(total, query, codes, flags, half_id, own_heads, buckets, bits, first)

    other0 = swapped(own_state, 1)
    own1 = swapped(block_sum, 2)
    total = local(None, True)
    other0, own1, total = lax.optimization_barrier((other0, own1, total))
    block_sum = block_sum + own1
    own2 = swapped(block_sum, 4)
    total = local(total, False)
    total = cross(total, True, [own0, own1], (0, 1))
    own2, total = lax.optimization_barrier((own2, total))
    block_sum = block_sum + own2
    own3, left, right = [swapped(block_sum, mask) for mask in (8, 16, 24)]
    total = cross(total, True, [own2], (2,))
    own1, own2, total = lax.optimization_barrier((own1, own2, total))
    low = swapped(jnp.concatenate([own1, own2], axis=0), 1)
    own3, left, right, total = lax.optimization_barrier((own3, left, right, total))
    own4 = left + right
    block_sum = block_sum + (own3 + own4)
    own5, left, right = [swapped(block_sum, mask) for mask in (32, 64, 96)]
    total = cross(total, True, [own3, own4], (3, 4))
    own3, own4, total = lax.optimization_barrier((own3, own4, total))
    other3 = swapped(own3, 1)
    other4 = next_along_z(own4)
    total = cross(total, False, [other0, low[:half], low[half:]], (0, 1, 2))
    own5, left, right, total = lax.optimization_barrier((own5, left, right, total))
    own6 = left + right
    other5 = swapped(own5, 1)
    other6 = next_along_z(own6)
    wide = finish_own(total, query, codes, flags, half_id, norm_gain, (own5, own6), (5, 6), first)
    total, wide = lax.optimization_barrier((total, wide))
    total = cross(total, False, [other3, other4], (3, 4))
    return finish_other(
        wide, total, query, codes, flags, half_id, norm_gain, (other5, other6), (5, 6), first
    )


def solution(mesh):
    return jax.shard_map(
        shards,
        mesh=mesh,
        in_specs=(
            P("seq", "head", None),
            P("seq", "head", None),
            P("seq", "head", None),
            P("head", None, "seq"),
            P("head", None),
        ),
        out_specs=P("seq", "head", None),
        check_vma=False,
    )
```

```python
import functools

import jax
import jax.numpy as jnp
import numpy as np
from jax import lax
from jax.experimental import pallas as pl
from jax.experimental.pallas import tpu as pltpu
from jax.sharding import PartitionSpec as P

STATES_MIB = 58
NT = (((1,), (1,)), ((), ()))
VMEM = pl.BlockSpec(memory_space=pltpu.VMEM)
SMEM = pl.BlockSpec(memory_space=pltpu.SMEM)
ANY = pl.BlockSpec(memory_space=pl.ANY)


def params(mib):
    return pltpu.CompilerParams(vmem_limit_bytes=mib * 1024 * 1024)


def cost(flops, nbytes):
    return pl.CostEstimate(flops=flops, bytes_accessed=nbytes, transcendentals=0)


def level_map(size):
    source = np.arange(size)[:, None]
    target = np.arange(size)[None, :]
    levels = np.zeros((size, size), np.int32)
    for shift in range(24):
        levels += (target >> shift != source >> shift).astype(np.int32)
    return np.where(source <= target, levels, -1).astype(np.int32)


def first_head(owner_ref, own_heads, half):
    return (owner_ref[0] if own_heads else 1 - owner_ref[0]) * half


def states_kernel(heads, rows, owner_ref, k_hbm, v_hbm, own_out, other_out, k_in, v_in, k_wide, v_wide, state, sems):
    chunks = k_in.shape[0]
    half = heads // 2

    def load(hbm, buffer, which, i):
        part = pl.ds(i * rows * heads, rows * heads)
        return pltpu.make_async_copy(hbm.at[part], buffer.at[i], sems.at[which, i])

    for i in range(chunks):
        load(k_hbm, k_in, 0, i).start()
        load(v_hbm, v_in, 1, i).start()
    for i in range(chunks):
        load(k_hbm, k_in, 0, i).wait()
        load(v_hbm, v_in, 1, i).wait()
        k_wide[...] = k_in[i].astype(jnp.float32)
        v_wide[...] = v_in[i].astype(jnp.float32)
        for h in range(heads):
            key = k_wide[pl.ds(h, rows, stride=heads), :].astype(jnp.bfloat16)
            value = v_wide[pl.ds(h, rows, stride=heads), :].T.astype(jnp.bfloat16)
            product = jnp.dot(value, key, preferred_element_type=jnp.float32)
            if i:
                product = state[h] + product
            state[h] = product
    owner = owner_ref[0]
    own_out[...] = state[pl.ds(owner * half, half)]
    other_out[...] = state[pl.ds((1 - owner) * half, half)]


def make_states(key_rows, value_rows, owner, rows=128):
    length, heads, dim = key_rows.shape
    chunks = length // rows
    part = jax.ShapeDtypeStruct((heads // 2, dim, dim), jnp.float32)
    return pl.pallas_call(
        functools.partial(states_kernel, heads, rows),
        in_specs=[SMEM, ANY, ANY],
        out_specs=[VMEM, VMEM],
        out_shape=[part, part],
        scratch_shapes=[pltpu.VMEM((chunks, rows * heads, dim), jnp.bfloat16)] * 2
        + [pltpu.VMEM((rows * heads, dim), jnp.float32)] * 2
        + [pltpu.VMEM((heads, dim, dim), jnp.float32)]
        + [pltpu.SemaphoreType.DMA((2, chunks))],
        compiler_params=params(STATES_MIB),
        cost_estimate=cost(2 * heads * length * dim * dim, 4 * length * heads * dim),
        name="states",
    )(owner, key_rows.reshape(length * heads, dim), value_rows.reshape(length * heads, dim))


def split_kernel(heads, rows, _, q_ref, k_ref, v_ref, q_out, k_out, v_out, q_wide, k_wide, v_wide):
    for i in range(q_out.shape[1] // rows):
        span = slice(i * rows, (i + 1) * rows)
        flat = slice(i * rows * heads, (i + 1) * rows * heads)
        q_wide[...] = q_ref[flat, :].astype(jnp.float32)
        k_wide[...] = k_ref[flat, :].astype(jnp.float32)
        v_wide[...] = v_ref[flat, :].astype(jnp.float32)
        for h in range(heads):
            q_out[h, span, :] = q_wide[pl.ds(h, rows, stride=heads), :].astype(jnp.bfloat16)
            k_out[h, span, :] = k_wide[pl.ds(h, rows, stride=heads), :].astype(jnp.bfloat16)
            v_out[h, :, span] = v_wide[pl.ds(h, rows, stride=heads), :].T.astype(jnp.bfloat16)


def split_heads(earlier, query_rows, key_rows, value_rows, rows=256):
    length, heads, dim = query_rows.shape
    straight = jax.ShapeDtypeStruct((heads, length, dim), jnp.bfloat16)
    turned = jax.ShapeDtypeStruct((heads, dim, length), jnp.bfloat16)
    return pl.pallas_call(
        functools.partial(split_kernel, heads, rows),
        in_specs=[ANY] + [VMEM] * 3,
        out_specs=[VMEM] * 3,
        out_shape=[straight, straight, turned],
        scratch_shapes=[pltpu.VMEM((rows * heads, dim), jnp.float32)] * 3,
        compiler_params=params(12),
        cost_estimate=cost(0, 12 * length * heads * dim),
        name="split_heads",
    )(earlier, *[each.reshape(length * heads, dim) for each in (query_rows, key_rows, value_rows)])


def local_kernel(length, tile, small, own_heads, owner_ref, q_ref, k_ref, v_ref, codes_ref, map_ref, *refs):
    out_ref = refs[-1]
    low_levels = small.bit_length()

    half = q_ref.shape[0] // 2
    begin = first_head(owner_ref, own_heads, half)

    @pl.loop(0, half)
    def _(i):
        h = begin + i
        weights = [codes_ref[level, pl.ds(h, 1), :].astype(jnp.float32) * (1.0 / 64.0) for level in range(length.bit_length())]
        levels = map_ref[...]
        masks = [levels == level for level in range(low_levels)]
        for t in range(length // tile):
            columns = slice(t * tile, (t + 1) * tile)
            count = (t + 1) * tile
            scores = lax.dot_general(
                k_ref[h, :count, :], q_ref[h, columns, :], NT, preferred_element_type=jnp.float32
            )
            pieces = []
            for s in range(t):
                level = (t ^ s).bit_length() + tile.bit_length() - 1
                piece = scores[s * tile:(s + 1) * tile] * weights[level][:, columns]
                pieces.append(piece.astype(jnp.bfloat16))
            for i in range(tile // small):
                row = []
                for j in range(tile // small):
                    first = t * tile + j * small
                    lanes = slice(first, first + small)
                    part = scores[t * tile + i * small:t * tile + (i + 1) * small, j * small:(j + 1) * small]
                    if j < i:
                        row.append(jnp.zeros((small, small), jnp.bfloat16))
                        continue
                    if j > i:
                        level = (i ^ j).bit_length() + small.bit_length() - 1
                        picked = weights[level][:, lanes]
                    else:
                        picked = jnp.zeros((small, small), jnp.float32)
                        for level in range(low_levels):
                            picked = jnp.where(masks[level], weights[level][:, lanes], picked)
                    row.append((part * picked).astype(jnp.bfloat16))
                pieces.append(jnp.concatenate(row, axis=1))
            weighted = jnp.concatenate(pieces, axis=0) if len(pieces) > 1 else pieces[0]
            out_ref[h, :, columns] = jnp.dot(
                v_ref[h, :, :count], weighted, preferred_element_type=jnp.float32
            )


def local_part(total, query, key, value, codes, owner, own_heads, tile=256, small=128):
    every, length, dim = query.shape
    operands = [owner, query, key, value, codes, jnp.asarray(level_map(small))]
    specs = [SMEM] + [VMEM] * (len(operands) - 1)
    aliases = {}
    if total is not None:
        aliases = {len(operands): 0}
        operands.append(total)
        specs.append(VMEM)
    return pl.pallas_call(
        functools.partial(local_kernel, length, tile, small, own_heads),
        in_specs=specs,
        out_specs=VMEM,
        out_shape=jax.ShapeDtypeStruct((every, dim, length), jnp.float32),
        input_output_aliases=aliases,
        compiler_params=params(12),
        cost_estimate=cost(5 * every * length * length * dim, 8 * length * every * dim),
        name="local_part",
    )(*operands)


def bucket_products(buckets, query):
    stacked = jnp.concatenate(buckets, axis=0) if len(buckets) > 1 else buckets[0]
    high = stacked.astype(jnp.bfloat16)
    low = (stacked - high.astype(jnp.float32)).astype(jnp.bfloat16)
    products = lax.dot_general(
        jnp.concatenate([high, low], axis=1),
        jnp.concatenate([query, query], axis=1),
        NT,
        preferred_element_type=jnp.float32,
    )
    dim = query.shape[1]
    return [products[i * dim:(i + 1) * dim] for i in range(len(buckets))]


def cross_kernel(bits, first, own_heads, owner_ref, flag_ref, total_ref, q_ref, codes_ref, *refs):
    out_ref = refs[-1]
    half = q_ref.shape[0] // 2
    begin = first_head(owner_ref, own_heads, half)

    @pl.loop(0, half)
    def _(i):
        h = begin + i
        total = total_ref[h]
        products = bucket_products([ref[i] for ref in refs[:-1]], q_ref[h])
        for product, bit in zip(products, bits):
            scale = codes_ref[first + bit, pl.ds(h, 1), :].astype(jnp.float32) * flag_ref[bit]
            total = total + scale * product
        out_ref[h] = total


def add_cross(total, query, codes, flags, owner, own_heads, buckets, bits, first):
    heads, length, dim = query.shape
    return pl.pallas_call(
        functools.partial(cross_kernel, bits, first, own_heads),
        in_specs=[SMEM, SMEM] + [VMEM] * (3 + len(bits)),
        out_specs=VMEM,
        out_shape=jax.ShapeDtypeStruct((heads, dim, length), jnp.float32),
        input_output_aliases={2: 0},
        compiler_params=params(12),
        cost_estimate=cost(3 * len(bits) * heads * length * dim * dim, 3 * length * heads * dim),
        name="add_cross",
    )(owner, flags, total, query, codes, *buckets)


def finish_kernel(bits, first, rows, own_heads, owner_ref, flag_ref, total_ref, q_ref, codes_ref, gain_ref, *refs):
    buckets = refs[:len(bits)]
    if own_heads:
        wide = refs[-1]
    else:
        wide, out_hbm, narrow, sems = refs[-4:]
    heads, dim, length = total_ref.shape
    half = heads // 2
    chunks = length // rows
    begin = first_head(owner_ref, own_heads, half)

    def store(i):
        part = pl.ds(i * rows * heads, rows * heads)
        return pltpu.make_async_copy(narrow.at[i], out_hbm.at[part], sems.at[i])

    for c in range(chunks):
        columns = slice(c * rows, (c + 1) * rows)
        for i in range(half):
            h = begin + i
            total = total_ref[h, :, columns]
            products = bucket_products([ref[i] for ref in buckets], q_ref[h, columns, :])
            for product, bit in zip(products, bits):
                scale = codes_ref[first + bit, pl.ds(h, 1), columns].astype(jnp.float32) * flag_ref[bit]
                total = total + scale * product
            mean_square = jnp.sum(total * total, axis=0, keepdims=True) * (1.0 / dim)
            normed = total * lax.rsqrt(mean_square + 1e-06)
            wide[pl.ds(c * rows * heads + h, rows, stride=heads), :] = normed.T * gain_ref[pl.ds(h, 1), :]
        if not own_heads:
            narrow[c] = wide[c * rows * heads:(c + 1) * rows * heads, :].astype(jnp.bfloat16)
            store(c).start()
    if not own_heads:
        for c in range(chunks):
            store(c).wait()


def finish_own(total, query, codes, flags, owner, gain, buckets, bits, first, rows=256):
    heads, length, dim = query.shape
    return pl.pallas_call(
        functools.partial(finish_kernel, bits, first, rows, True),
        in_specs=[SMEM, SMEM] + [VMEM] * (4 + len(bits)),
        out_specs=VMEM,
        out_shape=jax.ShapeDtypeStruct((length * heads, dim), jnp.float32),
        compiler_params=params(12),
        cost_estimate=cost(4 * heads * length * dim * dim, 4 * length * heads * dim),
        name="finish_own",
    )(owner, flags, total, query, codes, gain, *buckets)


def finish_other(wide, total, query, codes, flags, owner, gain, buckets, bits, first, rows=256):
    heads, length, dim = query.shape
    _, out = pl.pallas_call(
        functools.partial(finish_kernel, bits, first, rows, False),
        in_specs=[SMEM, SMEM] + [VMEM] * (5 + len(bits)),
        out_specs=[VMEM, ANY],
        out_shape=[
            jax.ShapeDtypeStruct((length * heads, dim), jnp.float32),
            jax.ShapeDtypeStruct((length * heads, dim), jnp.bfloat16),
        ],
        scratch_shapes=[
            pltpu.VMEM((length // rows, rows * heads, dim), jnp.bfloat16),
            pltpu.SemaphoreType.DMA((length // rows,)),
        ],
        input_output_aliases={6 + len(bits): 0},
        compiler_params=params(12),
        cost_estimate=cost(4 * heads * length * dim * dim, 10 * length * heads * dim),
        name="finish_other",
    )(owner, flags, total, query, codes, gain, *buckets, wide)
    return out.reshape(length, heads, dim)


def swapped(block, mask):
    count = lax.axis_size("seq")
    return lax.ppermute(block, "seq", [(i, i ^ mask) for i in range(count)])


def next_along_z(block):
    count = lax.axis_size("seq")
    route = []
    for i in range(count):
        ring = i & ~7
        step = 1 if i & 1 else -1
        route.append((i, ring | (i + step) & 7))
    return lax.ppermute(block, "seq", route)


def shards(query_rows, key_rows, value_rows, level_codes, norm_gain):
    bit_count = lax.axis_size("seq").bit_length() - 1
    first = level_codes.shape[1] - bit_count
    position = lax.axis_index("seq")
    bits = jnp.arange(bit_count, dtype=jnp.int32)
    flags = (position >> bits & 1).astype(jnp.float32) * (1.0 / 64.0)
    owner = position & 1
    half_id = owner.reshape(1).astype(jnp.int32)

    codes = jnp.transpose(level_codes, (1, 0, 2))
    own_state, other_state = make_states(key_rows, value_rows, half_id)
    half = own_state.shape[0]

    own0 = swapped(other_state, 1)
    query, key, value = split_heads(own_state, query_rows, key_rows, value_rows)
    own0, own_state, query = lax.optimization_barrier((own0, own_state, query))
    block_sum = own_state + own0

    def local(total, own_heads):
        return local_part(total, query, key, value, codes, half_id, own_heads)

    def cross(total, own_heads, buckets, bits):
        return add_cross(total, query, codes, flags, half_id, own_heads, buckets, bits, first)

    other0 = swapped(own_state, 1)
    own1 = swapped(block_sum, 2)
    total = local(None, True)
    other0, own1, total = lax.optimization_barrier((other0, own1, total))
    block_sum = block_sum + own1
    own2 = swapped(block_sum, 6)
    total = local(total, False)
    total = cross(total, True, [own0, own1], (0, 1))
    own2, total = lax.optimization_barrier((own2, total))
    block_sum = block_sum + own2
    own3, left, right = [swapped(block_sum, mask) for mask in (8, 16, 24)]
    total = cross(total, True, [own2], (2,))
    own1, own2, total = lax.optimization_barrier((own1, own2, total))
    low = swapped(jnp.concatenate([own1, own2], axis=0), 1)
    own3, left, right, total = lax.optimization_barrier((own3, left, right, total))
    own4 = left + right
    block_sum = block_sum + (own3 + own4)
    own5, left, right = [swapped(block_sum, mask) for mask in (32, 64, 96)]
    total = cross(total, True, [own3, own4], (3, 4))
    own3, own4, total = lax.optimization_barrier((own3, own4, total))
    other3 = swapped(own3, 1)
    other4 = next_along_z(own4)
    total = cross(total, False, [other0, low[:half], low[half:]], (0, 1, 2))
    own5, left, right, total = lax.optimization_barrier((own5, left, right, total))
    own6 = left + right
    other5 = swapped(own5, 1)
    other6 = next_along_z(own6)
    wide = finish_own(total, query, codes, flags, half_id, norm_gain, (own5, own6), (5, 6), first)
    total, wide = lax.optimization_barrier((total, wide))
    total = cross(total, False, [other3, other4], (3, 4))
    return finish_other(
        wide, total, query, codes, flags, half_id, norm_gain, (other5, other6), (5, 6), first
    )


def solution(mesh):
    return jax.shard_map(
        shards,
        mesh=mesh,
        in_specs=(
            P("seq", "head", None),
            P("seq", "head", None),
            P("seq", "head", None),
            P("head", None, "seq"),
            P("head", None),
        ),
        out_specs=P("seq", "head", None),
        check_vma=False,
    )
```

```python
import functools

import jax
import jax.numpy as jnp
import numpy as np
from jax import lax
from jax.experimental import pallas as pl
from jax.experimental.pallas import tpu as pltpu
from jax.sharding import PartitionSpec as P

STATES_MIB = 58
NT = (((1,), (1,)), ((), ()))
VMEM = pl.BlockSpec(memory_space=pltpu.VMEM)
SMEM = pl.BlockSpec(memory_space=pltpu.SMEM)
ANY = pl.BlockSpec(memory_space=pl.ANY)


def params(mib):
    return pltpu.CompilerParams(vmem_limit_bytes=mib * 1024 * 1024)


def cost(flops, nbytes):
    return pl.CostEstimate(flops=flops, bytes_accessed=nbytes, transcendentals=0)


def level_map(size):
    source = np.arange(size)[:, None]
    target = np.arange(size)[None, :]
    levels = np.zeros((size, size), np.int32)
    for shift in range(24):
        levels += (target >> shift != source >> shift).astype(np.int32)
    return np.where(source <= target, levels, -1).astype(np.int32)


def first_head(owner_ref, own_heads, half):
    return (owner_ref[0] if own_heads else 1 - owner_ref[0]) * half


def states_kernel(heads, rows, owner_ref, k_hbm, v_hbm, own_out, other_out, k_in, v_in, k_wide, v_wide, state, sems):
    chunks = k_in.shape[0]
    half = heads // 2

    def load(hbm, buffer, which, i):
        part = pl.ds(i * rows * heads, rows * heads)
        return pltpu.make_async_copy(hbm.at[part], buffer.at[i], sems.at[which, i])

    for i in range(chunks):
        load(k_hbm, k_in, 0, i).start()
        load(v_hbm, v_in, 1, i).start()
    for i in range(chunks):
        load(k_hbm, k_in, 0, i).wait()
        load(v_hbm, v_in, 1, i).wait()
        k_wide[...] = k_in[i].astype(jnp.float32)
        v_wide[...] = v_in[i].astype(jnp.float32)
        for h in range(heads):
            key = k_wide[pl.ds(h, rows, stride=heads), :].astype(jnp.bfloat16)
            value = v_wide[pl.ds(h, rows, stride=heads), :].T.astype(jnp.bfloat16)
            product = jnp.dot(value, key, preferred_element_type=jnp.float32)
            if i:
                product = state[h] + product
            state[h] = product
    owner = owner_ref[0]
    own_out[...] = state[pl.ds(owner * half, half)]
    other_out[...] = state[pl.ds((1 - owner) * half, half)]


def make_states(key_rows, value_rows, owner, rows=128):
    length, heads, dim = key_rows.shape
    chunks = length // rows
    part = jax.ShapeDtypeStruct((heads // 2, dim, dim), jnp.float32)
    return pl.pallas_call(
        functools.partial(states_kernel, heads, rows),
        in_specs=[SMEM, ANY, ANY],
        out_specs=[VMEM, VMEM],
        out_shape=[part, part],
        scratch_shapes=[pltpu.VMEM((chunks, rows * heads, dim), jnp.bfloat16)] * 2
        + [pltpu.VMEM((rows * heads, dim), jnp.float32)] * 2
        + [pltpu.VMEM((heads, dim, dim), jnp.float32)]
        + [pltpu.SemaphoreType.DMA((2, chunks))],
        compiler_params=params(STATES_MIB),
        cost_estimate=cost(2 * heads * length * dim * dim, 4 * length * heads * dim),
        name="states",
    )(owner, key_rows.reshape(length * heads, dim), value_rows.reshape(length * heads, dim))


def split_kernel(heads, rows, _, q_ref, k_ref, v_ref, q_out, k_out, v_out, q_wide, k_wide, v_wide):
    for i in range(q_out.shape[1] // rows):
        span = slice(i * rows, (i + 1) * rows)
        flat = slice(i * rows * heads, (i + 1) * rows * heads)
        q_wide[...] = q_ref[flat, :].astype(jnp.float32)
        k_wide[...] = k_ref[flat, :].astype(jnp.float32)
        v_wide[...] = v_ref[flat, :].astype(jnp.float32)
        for h in range(heads):
            q_out[h, span, :] = q_wide[pl.ds(h, rows, stride=heads), :].astype(jnp.bfloat16)
            k_out[h, span, :] = k_wide[pl.ds(h, rows, stride=heads), :].astype(jnp.bfloat16)
            v_out[h, :, span] = v_wide[pl.ds(h, rows, stride=heads), :].T.astype(jnp.bfloat16)


def split_heads(earlier, query_rows, key_rows, value_rows, rows=256):
    length, heads, dim = query_rows.shape
    straight = jax.ShapeDtypeStruct((heads, length, dim), jnp.bfloat16)
    turned = jax.ShapeDtypeStruct((heads, dim, length), jnp.bfloat16)
    return pl.pallas_call(
        functools.partial(split_kernel, heads, rows),
        in_specs=[ANY] + [VMEM] * 3,
        out_specs=[VMEM] * 3,
        out_shape=[straight, straight, turned],
        scratch_shapes=[pltpu.VMEM((rows * heads, dim), jnp.float32)] * 3,
        compiler_params=params(12),
        cost_estimate=cost(0, 12 * length * heads * dim),
        name="split_heads",
    )(earlier, *[each.reshape(length * heads, dim) for each in (query_rows, key_rows, value_rows)])


def local_kernel(length, tile, small, own_heads, owner_ref, q_ref, k_ref, v_ref, codes_ref, map_ref, *refs):
    out_ref = refs[-1]
    low_levels = small.bit_length()

    half = q_ref.shape[0] // 2
    begin = first_head(owner_ref, own_heads, half)

    @pl.loop(0, half)
    def _(i):
        h = begin + i
        weights = [codes_ref[level, pl.ds(h, 1), :].astype(jnp.float32) * (1.0 / 64.0) for level in range(length.bit_length())]
        levels = map_ref[...]
        masks = [levels == level for level in range(low_levels)]
        for t in range(length // tile):
            columns = slice(t * tile, (t + 1) * tile)
            count = (t + 1) * tile
            scores = lax.dot_general(
                k_ref[h, :count, :], q_ref[h, columns, :], NT, preferred_element_type=jnp.float32
            )
            pieces = []
            for s in range(t):
                level = (t ^ s).bit_length() + tile.bit_length() - 1
                piece = scores[s * tile:(s + 1) * tile] * weights[level][:, columns]
                pieces.append(piece.astype(jnp.bfloat16))
            for i in range(tile // small):
                row = []
                for j in range(tile // small):
                    first = t * tile + j * small
                    lanes = slice(first, first + small)
                    part = scores[t * tile + i * small:t * tile + (i + 1) * small, j * small:(j + 1) * small]
                    if j < i:
                        row.append(jnp.zeros((small, small), jnp.bfloat16))
                        continue
                    if j > i:
                        level = (i ^ j).bit_length() + small.bit_length() - 1
                        picked = weights[level][:, lanes]
                    else:
                        picked = jnp.zeros((small, small), jnp.float32)
                        for level in range(low_levels):
                            picked = jnp.where(masks[level], weights[level][:, lanes], picked)
                    row.append((part * picked).astype(jnp.bfloat16))
                pieces.append(jnp.concatenate(row, axis=1))
            weighted = jnp.concatenate(pieces, axis=0) if len(pieces) > 1 else pieces[0]
            out_ref[h, :, columns] = jnp.dot(
                v_ref[h, :, :count], weighted, preferred_element_type=jnp.float32
            )


def local_part(total, query, key, value, codes, owner, own_heads, tile=256, small=128):
    every, length, dim = query.shape
    operands = [owner, query, key, value, codes, jnp.asarray(level_map(small))]
    specs = [SMEM] + [VMEM] * (len(operands) - 1)
    aliases = {}
    if total is not None:
        aliases = {len(operands): 0}
        operands.append(total)
        specs.append(VMEM)
    return pl.pallas_call(
        functools.partial(local_kernel, length, tile, small, own_heads),
        in_specs=specs,
        out_specs=VMEM,
        out_shape=jax.ShapeDtypeStruct((every, dim, length), jnp.float32),
        input_output_aliases=aliases,
        compiler_params=params(12),
        cost_estimate=cost(5 * every * length * length * dim, 8 * length * every * dim),
        name="local_part",
    )(*operands)


def bucket_products(buckets, query):
    stacked = jnp.concatenate(buckets, axis=0) if len(buckets) > 1 else buckets[0]
    high = stacked.astype(jnp.bfloat16)
    low = (stacked - high.astype(jnp.float32)).astype(jnp.bfloat16)
    products = lax.dot_general(
        jnp.concatenate([high, low], axis=1),
        jnp.concatenate([query, query], axis=1),
        NT,
        preferred_element_type=jnp.float32,
    )
    dim = query.shape[1]
    return [products[i * dim:(i + 1) * dim] for i in range(len(buckets))]


def cross_kernel(bits, first, own_heads, owner_ref, flag_ref, total_ref, q_ref, codes_ref, *refs):
    out_ref = refs[-1]
    half = q_ref.shape[0] // 2
    begin = first_head(owner_ref, own_heads, half)

    @pl.loop(0, half)
    def _(i):
        h = begin + i
        total = total_ref[h]
        products = bucket_products([ref[i] for ref in refs[:-1]], q_ref[h])
        for product, bit in zip(products, bits):
            scale = codes_ref[first + bit, pl.ds(h, 1), :].astype(jnp.float32) * flag_ref[bit]
            total = total + scale * product
        out_ref[h] = total


def add_cross(total, query, codes, flags, owner, own_heads, buckets, bits, first):
    heads, length, dim = query.shape
    return pl.pallas_call(
        functools.partial(cross_kernel, bits, first, own_heads),
        in_specs=[SMEM, SMEM] + [VMEM] * (3 + len(bits)),
        out_specs=VMEM,
        out_shape=jax.ShapeDtypeStruct((heads, dim, length), jnp.float32),
        input_output_aliases={2: 0},
        compiler_params=params(12),
        cost_estimate=cost(3 * len(bits) * heads * length * dim * dim, 3 * length * heads * dim),
        name="add_cross",
    )(owner, flags, total, query, codes, *buckets)


def finish_kernel(bits, first, rows, own_heads, owner_ref, flag_ref, total_ref, q_ref, codes_ref, gain_ref, *refs):
    buckets = refs[:len(bits)]
    if own_heads:
        wide = refs[-1]
    else:
        wide, out_hbm, narrow, sems = refs[-4:]
    heads, dim, length = total_ref.shape
    half = heads // 2
    chunks = length // rows
    begin = first_head(owner_ref, own_heads, half)

    def store(i):
        part = pl.ds(i * rows * heads, rows * heads)
        return pltpu.make_async_copy(narrow.at[i], out_hbm.at[part], sems.at[i])

    for c in range(chunks):
        columns = slice(c * rows, (c + 1) * rows)
        for i in range(half):
            h = begin + i
            total = total_ref[h, :, columns]
            products = bucket_products([ref[i] for ref in buckets], q_ref[h, columns, :])
            for product, bit in zip(products, bits):
                scale = codes_ref[first + bit, pl.ds(h, 1), columns].astype(jnp.float32) * flag_ref[bit]
                total = total + scale * product
            mean_square = jnp.sum(total * total, axis=0, keepdims=True) * (1.0 / dim)
            normed = total * lax.rsqrt(mean_square + 1e-06)
            wide[pl.ds(c * rows * heads + h, rows, stride=heads), :] = normed.T * gain_ref[pl.ds(h, 1), :]
        if not own_heads:
            narrow[c] = wide[c * rows * heads:(c + 1) * rows * heads, :].astype(jnp.bfloat16)
            store(c).start()
    if not own_heads:
        for c in range(chunks):
            store(c).wait()


def finish_own(total, query, codes, flags, owner, gain, buckets, bits, first, rows=256):
    heads, length, dim = query.shape
    return pl.pallas_call(
        functools.partial(finish_kernel, bits, first, rows, True),
        in_specs=[SMEM, SMEM] + [VMEM] * (4 + len(bits)),
        out_specs=VMEM,
        out_shape=jax.ShapeDtypeStruct((length * heads, dim), jnp.float32),
        compiler_params=params(12),
        cost_estimate=cost(4 * heads * length * dim * dim, 4 * length * heads * dim),
        name="finish_own",
    )(owner, flags, total, query, codes, gain, *buckets)


def finish_other(wide, total, query, codes, flags, owner, gain, buckets, bits, first, rows=256):
    heads, length, dim = query.shape
    _, out = pl.pallas_call(
        functools.partial(finish_kernel, bits, first, rows, False),
        in_specs=[SMEM, SMEM] + [VMEM] * (5 + len(bits)),
        out_specs=[VMEM, ANY],
        out_shape=[
            jax.ShapeDtypeStruct((length * heads, dim), jnp.float32),
            jax.ShapeDtypeStruct((length * heads, dim), jnp.bfloat16),
        ],
        scratch_shapes=[
            pltpu.VMEM((length // rows, rows * heads, dim), jnp.bfloat16),
            pltpu.SemaphoreType.DMA((length // rows,)),
        ],
        input_output_aliases={6 + len(bits): 0},
        compiler_params=params(12),
        cost_estimate=cost(4 * heads * length * dim * dim, 10 * length * heads * dim),
        name="finish_other",
    )(owner, flags, total, query, codes, gain, *buckets, wide)
    return out.reshape(length, heads, dim)


def swapped(block, mask):
    count = lax.axis_size("seq")
    return lax.ppermute(block, "seq", [(i, i ^ mask) for i in range(count)])


def next_along_z(block):
    count = lax.axis_size("seq")
    route = []
    for i in range(count):
        ring = i & ~7
        step = 1 if i & 1 else -1
        route.append((i, ring | (i + step) & 7))
    return lax.ppermute(block, "seq", route)


def shards(query_rows, key_rows, value_rows, level_codes, norm_gain):
    bit_count = lax.axis_size("seq").bit_length() - 1
    first = level_codes.shape[1] - bit_count
    position = lax.axis_index("seq")
    bits = jnp.arange(bit_count, dtype=jnp.int32)
    flags = (position >> bits & 1).astype(jnp.float32) * (1.0 / 64.0)
    owner = position & 1
    half_id = owner.reshape(1).astype(jnp.int32)

    codes = jnp.transpose(level_codes, (1, 0, 2))
    own_state, other_state = make_states(key_rows, value_rows, half_id)
    half = own_state.shape[0]

    own0 = swapped(other_state, 1)
    query, key, value = split_heads(own_state, query_rows, key_rows, value_rows)
    own0, own_state, query = lax.optimization_barrier((own0, own_state, query))
    block_sum = own_state + own0

    def local(total, own_heads):
        return local_part(total, query, key, value, codes, half_id, own_heads)

    def cross(total, own_heads, buckets, bits):
        return add_cross(total, query, codes, flags, half_id, own_heads, buckets, bits, first)

    other0 = swapped(own_state, 1)
    own1 = swapped(block_sum, 2)
    total = local(None, True)
    other0, own1, total = lax.optimization_barrier((other0, own1, total))
    block_sum = block_sum + own1
    own2 = swapped(block_sum, 6)
    other1 = swapped(own1, 1)
    total = local(total, False)
    total = cross(total, True, [own0, own1], (0, 1))
    other1, own2, total = lax.optimization_barrier((other1, own2, total))
    block_sum = block_sum + own2
    own3, left, right = [swapped(block_sum, mask) for mask in (8, 16, 24)]
    total = cross(total, True, [own2], (2,))
    own2, total = lax.optimization_barrier((own2, total))
    other2 = swapped(own2, 1)
    own3, left, right, total = lax.optimization_barrier((own3, left, right, total))
    own4 = left + right
    block_sum = block_sum + (own3 + own4)
    own5, left, right = [swapped(block_sum, mask) for mask in (32, 64, 96)]
    total = cross(total, True, [own3, own4], (3, 4))
    own3, own4, total = lax.optimization_barrier((own3, own4, total))
    other3 = swapped(own3, 1)
    other4 = next_along_z(own4)
    total = cross(total, False, [other0, other1, other2], (0, 1, 2))
    own5, left, right, total = lax.optimization_barrier((own5, left, right, total))
    own6 = left + right
    other5 = swapped(own5, 1)
    other6 = next_along_z(own6)
    wide = finish_own(total, query, codes, flags, half_id, norm_gain, (own5, own6), (5, 6), first)
    total, wide = lax.optimization_barrier((total, wide))
    total = cross(total, False, [other3, other4], (3, 4))
    return finish_other(
        wide, total, query, codes, flags, half_id, norm_gain, (other5, other6), (5, 6), first
    )


def solution(mesh):
    return jax.shard_map(
        shards,
        mesh=mesh,
        in_specs=(
            P("seq", "head", None),
            P("seq", "head", None),
            P("seq", "head", None),
            P("head", None, "seq"),
            P("head", None),
        ),
        out_specs=P("seq", "head", None),
        check_vma=False,
    )
```
